256 devices in a mesh: row: 8 (over z_hi, x), col: 32 (over z_lo, y, core).
Axes of the slice: x: 4, y: 4, z: 8 (z_hi: 2, z_lo: 4; z = z_hi * 4 + z_lo), core: 2. Of those that a mesh axis runs over, the one named last changes fastest.
Arguments:
- lower_panel: float32 [3, 16384, 256], P(None, ('row', 'col')), may hold values from -6 to 6
- panel_mask: int32 [3, 128], P(None, 'row'), may hold values 0 or 1
- inverse_tiles: float32 [3, 16384, 16384], P(None, 'col', 'row'), may hold values from -0.125 to 0.125
- tile_mask: int32 [3, 128, 128], P(None, 'col', 'row'), may hold values from 0 to 1, as said below
Outputs:
- inverse_panel: float32 [3, 16384, 256], P(None, ('col', 'row'))
The draws below stay inside these ranges and needn't reach their ends.
Inputs may be any that keep to these rules, and one draw needn't show every extreme that they name: `tile_mask`: 1 marks a present block, 0 an absent one; the share of present blocks differs from block row to block row.
All inputs are finite; a program needn't handle non-finite values. No bound on the sum of `panel_mask` on one device may be relied on, other than what follows from the above.
Results may differ from the reference program's by a relative error of at most 0.00007.
Values sent between devices are 32-bit elements; how exact they have to be, the bound alone decides.
No kernel may reach another device: no remote copies, remote signals or barrier semaphores. Data moves between devices by JAX's collectives and lax.ppermute only.
A program may use at most 128 MiB of HBM per device.

```python
import jax
import jax.numpy as jnp
from jax import lax

W = 256
BLK = 128
SNODES = 3
S = 16384
N_COL = 32


def draw_tile_mask(key, part):
    key = jax.random.fold_in(key, 11)
    first_key, second_key = jax.random.split(key)
    row_level = jax.random.randint(first_key, (SNODES, S // BLK, 1), 2, 9)
    uniform_ints = jax.random.randint(second_key, (SNODES, S // BLK, S // BLK), 0, 8)
    return (uniform_ints < row_level).astype(jnp.int32)


def touch_ends(array, own_key, least, largest):
    spot = [jax.random.randint(jax.random.fold_in(own_key, axis), (), 0, length) for axis, length in enumerate(array.shape)]
    main_axis = array.shape.index(max(array.shape))
    neighbour = spot[:main_axis] + [(spot[main_axis] + 1) % array.shape[main_axis]] + spot[main_axis + 1:]
    return array.at[tuple(spot)].set(least).at[tuple(neighbour)].set(largest)


def strengthened(array, rng, source, target, blocks, factor):
    def block_of(position):
        return (jnp.arange(array.shape[position]) // (array.shape[position] // blocks)).reshape((-1,) + (1,) * (array.ndim - 1 - position))

    first = jax.random.permutation(rng, blocks)[block_of(target)]
    second = (block_of(target) + blocks // 2) % blocks
    return jnp.where((block_of(source) == first) | (block_of(source) == second), factor * array, array)


def levels(key, shape, cuts, least, high):
    gain, own = 1.0, jax.random.fold_in(key, 6)
    for axis_at, shards_of in cuts:
        heights = jnp.exp(jax.random.uniform(jax.random.fold_in(own, axis_at), (shards_of,), jnp.float32, least / len(cuts), high / len(cuts)))
        gain = gain * jnp.repeat(heights, shape[axis_at] // shards_of).reshape([-1 if axis == axis_at else 1 for axis in range(len(shape))])
    return gain


def gaussian(key, dims, spread, limit, shards=(), kind=jnp.bfloat16):
    values = spread * jax.random.normal(key, dims, jnp.float32)
    if shards:
        values = values * levels(key, dims, shards, -0.22, 0.18)
    return jnp.clip(values, -limit, limit).astype(kind)


def bell_draw_with(rng, dims, spread, bound, cuts, heavy, held_as=jnp.bfloat16):
    array = spread * jax.random.normal(rng, dims, jnp.float32)
    if cuts:
        array = array * levels(rng, dims, cuts, -0.22, 0.18)
    return jnp.clip(strengthened(array, jax.random.fold_in(rng, 3), *heavy), -bound, bound).astype(held_as)


def setup_inputs(seed: int = 0) -> dict:
    streams_of = jax.random.split(jax.random.key(seed), 5)
    return {
        "lower_panel": gaussian(streams_of[0], (SNODES, S, W), 1.0, 6.0, ((1, 256),), jnp.float32),
        "panel_mask": touch_ends((jax.random.randint(streams_of[1], (SNODES, S // BLK), 0, 4) < 3).astype(jnp.int32), jax.random.fold_in(streams_of[1], 1), 0, 1),
        "inverse_tiles": bell_draw_with(streams_of[2], (SNODES, S, S), (S // 2) ** -0.5, 0.125, ((1, 32), (2, 8)), (2, 1, 32, 2.75), jnp.float32),
        "tile_mask": draw_tile_mask(jax.random.fold_in(streams_of[4], 71), 0),
    }


def expand_tiles(values, flags):
    height, breadth = values.shape
    shaped = values.reshape(flags.shape[0], height // flags.shape[0], flags.shape[1], breadth // flags.shape[1])
    return (shaped * flags.astype(jnp.float32)[:, None, :, None]).reshape(height, breadth)


def one_snode(inputs):
    panel_one, flags_one, tiles_one, tile_flags = inputs
    total_rows = panel_one.shape[0]
    kept_panel = (panel_one.reshape(total_rows // BLK, BLK, W) * flags_one.astype(jnp.float32)[:, None, None]).reshape(total_rows, W)
    band_rows = total_rows // N_COL

    def band(items):
        tile_band, flag_band = items
        kept = expand_tiles(tile_band, flag_band)
        return -jnp.dot(kept, kept_panel, precision=lax.Precision.HIGHEST, preferred_element_type=jnp.float32)

    bands = lax.map(band, (tiles_one.reshape(N_COL, band_rows, total_rows), tile_flags.reshape(N_COL, band_rows // BLK, total_rows // BLK)))
    return bands.reshape(total_rows, W)


def reference(lower_panel, panel_mask, inverse_tiles, tile_mask):
    return lax.map(one_snode, (lower_panel, panel_mask, inverse_tiles, tile_mask))
```

```python
import functools

import jax
import jax.numpy as jnp
from jax import lax
from jax.experimental import pallas as pl
from jax.experimental.pallas import tpu as pltpu
from jax.sharding import Mesh
from jax.sharding import PartitionSpec as P

AXES = ("zh", "x", "zl", "y", "core")
SIZES = (2, 4, 4, 4, 2)
BLK = 128
MIB = 1 << 20


def shift(value, axis, by):
    size = SIZES[AXES.index(axis)]
    return lax.ppermute(value, axis, [(i, (i + by) % size) for i in range(size)])


def split(value):
    high = value.astype(jnp.bfloat16)
    low = (value - high.astype(jnp.float32)).astype(jnp.bfloat16)
    return high, low


def tiles_kernel(spot, tiles, factors, high, low):
    high[0], low[0] = split(tiles[0] * factors[0, 0])


def split_tiles(spot, tiles, factors):
    number, height, breadth = tiles.shape
    rows = height // 8

    def chunk(n, i, spot):
        zh = (spot[0] + i % 2) % 2
        x = (spot[1] + i // 2) % 4
        return zh * 4 + x

    out = jax.ShapeDtypeStruct(tiles.shape, jnp.bfloat16)
    out_spec = pl.BlockSpec((1, rows, breadth), lambda n, i, spot: (n, i, 0))
    return pl.pallas_call(
        tiles_kernel,
        out_shape=[out, out],
        grid_spec=pltpu.PrefetchScalarGridSpec(
            num_scalar_prefetch=1,
            grid=(number, 8),
            in_specs=[
                pl.BlockSpec((1, rows, breadth), lambda n, i, spot: (n, chunk(n, i, spot), 0)),
                pl.BlockSpec((1, 1, 1, breadth), lambda n, i, spot: (n, chunk(n, i, spot) // 2, 0, 0)),
            ],
            out_specs=[out_spec, out_spec],
        ),
        compiler_params=pltpu.CompilerParams(vmem_limit_bytes=8 * MIB),
        name="split_tiles",
    )(spot, tiles, factors)


def product_kernel(places, count, spot, high, low, *refs):
    pieces, outs, (panel_high, panel_low) = refs[:count], refs[count:-2], refs[-2:]
    zl, y, core = spot[2], spot[3], spot[4]
    for piece, place in zip(pieces, places):
        for part, (dz, dy, dc) in enumerate(place):
            block = (((zl + dz) % 4) * 4 + (y + dy) % 4) * 2 + (core + dc) % 2
            rows = pl.ds(pl.multiple_of(block * 64, 64), 64)
            hi, lo = split(piece[pl.ds(part * 64, 64), :])
            panel_high[rows, :] = hi
            panel_low[rows, :] = lo
    dot = functools.partial(jnp.dot, preferred_element_type=jnp.float32)
    step = high.shape[1] // 2
    for half in range(2):
        rows = pl.ds(half * step, step)
        total = dot(low[0, rows, :], panel_high[...])
        total += dot(high[0, rows, :], panel_low[...])
        total += dot(high[0, rows, :], panel_high[...])
        outs[2 * half][...] = total[:BLK]
        outs[2 * half + 1][...] = total[BLK:]


def product(n, spot, high, low, pieces, places):
    height, breadth = high.shape[1:]
    width = pieces[0].shape[1]
    whole = pl.BlockSpec(memory_space=pltpu.VMEM)
    tile_spec = pl.BlockSpec((1, height, breadth), lambda i, spot: (n, 0, 0))
    return pl.pallas_call(
        functools.partial(product_kernel, places, len(pieces)),
        out_shape=[jax.ShapeDtypeStruct((height // 4, width), jnp.float32)] * 4,
        grid_spec=pltpu.PrefetchScalarGridSpec(
            num_scalar_prefetch=1,
            grid=(1,),
            in_specs=[tile_spec, tile_spec] + [whole] * len(pieces),
            out_specs=[whole] * 4,
            scratch_shapes=[pltpu.VMEM((breadth, width), jnp.bfloat16)] * 2,
        ),
        compiler_params=pltpu.CompilerParams(vmem_limit_bytes=26 * MIB),
        name="product",
    )(spot, high, low, *pieces)


def local(lower_panel, panel_mask, inverse_tiles, tile_mask):
    number = lower_panel.shape[0]
    spot = jnp.stack([lax.axis_index(a) for a in AXES]).astype(jnp.int32)
    factors = -(tile_mask * panel_mask[:, None, :]).astype(jnp.float32)
    factors = jnp.repeat(factors, BLK, axis=2)[:, :, None, :]
    high, low = split_tiles(spot, inverse_tiles, factors)
    results = []
    for n in range(number):
        own = lower_panel[n]
        z1, z2, z3 = (shift(own, "zl", k) for k in (1, 2, 3))
        ga = jnp.concatenate([own, z1])
        gb = jnp.concatenate([z2, z3])
        pa, pb = shift(ga, "y", 1), shift(gb, "y", 1)
        ma, mb = shift(ga, "y", -1), shift(gb, "y", -1)
        qa, qb = shift(pa, "y", 1), shift(mb, "y", -1)
        mine = [ga, gb, pa, pb, ma, mb, qa, qb]
        pa_z, pb_z = (0, -1), (-2, -3)
        spots = [(pa_z, 0), (pb_z, 0), (pa_z, -1), (pb_z, -1), (pa_z, 1), (pb_z, 1), (pa_z, -2), (pb_z, 2)]
        other = [shift(v, "core", 1) for v in mine]
        places = [[(z % 4, dy % 4, dc) for z in zs] for dc in range(2) for zs, dy in spots]
        outs = product(n, spot, high, low, mine + other, places)
        total = outs[0]
        for k in (1, 2, 3):
            total = total + shift(outs[k], "x", k)
        results.append(total[:64] + shift(total[64:], "zh", 1))
    return jnp.stack(results)


def solution(mesh):
    mesh = Mesh(mesh.devices.reshape(SIZES), AXES)
    row, col = AXES[:2], AXES[2:]
    return jax.shard_map(
        local,
        mesh=mesh,
        in_specs=(P(None, AXES, None), P(None, row), P(None, col, row), P(None, col, row)),
        out_specs=P(None, col + row, None),
        check_vma=False,
    )
```

```python
import functools

import jax
import jax.numpy as jnp
from jax import lax
from jax.experimental import pallas as pl
from jax.experimental.pallas import tpu as pltpu
from jax.sharding import Mesh
from jax.sharding import PartitionSpec as P

AXES = ("zh", "x", "zl", "y", "core")
SIZES = (2, 4, 4, 4, 2)
BLK = 128
MIB = 1 << 20


def swap(value, axis, by, name):
    pairs = [(2 * i + core, 2 * (i ^ by[core]) + core) for i in range(SIZES[AXES.index(axis)]) for core in range(2)]
    with jax.named_scope(name):
        return lax.ppermute(value, (axis, "core"), pairs)


def swap_core(value, name):
    with jax.named_scope(name):
        return lax.ppermute(value, "core", [(0, 1), (1, 0)])


def split(value):
    high = value.astype(jnp.bfloat16)
    low = (value - high.astype(jnp.float32)).astype(jnp.bfloat16)
    return high, low


def ring_order(core):
    return [0, 1 + 2 * core, 3 - 2 * core, 2]


def tiles_kernel(spot, factors, tiles, high, low, held, arrived):
    zh, x, core = spot[0], spot[1], spot[4]
    own, first, second, both = ring_order(core)
    sources = [(zh ^ dz) * 4 + (x ^ dx) for dx in (own, second, first, both) for dz in range(2)]
    number, height, _ = tiles.shape
    rows = height // len(sources)

    def copy(n, i):
        rows_from = pl.ds(pl.multiple_of(sources[i] * rows, rows), rows)
        return pltpu.make_async_copy(tiles.at[n, rows_from], held.at[n, pl.ds(i * rows, rows)], arrived.at[n, i])

    @pl.loop(0, number)
    def _(n):
        for i in range(len(sources)):
            copy(n, i).start()

    @pl.loop(0, number)
    def _(n):
        for i, source in enumerate(sources):
            copy(n, i).wait()
            to = pl.ds(i * rows, rows)
            high[n, to], low[n, to] = split(held[n, to] * factors[n, source // 2])


def split_tiles(spot, tiles, factors):
    out = jax.ShapeDtypeStruct(tiles.shape, jnp.bfloat16)
    whole = pl.BlockSpec(memory_space=pltpu.VMEM)
    return pl.pallas_call(
        tiles_kernel,
        out_shape=[out, out],
        in_specs=[pl.BlockSpec(memory_space=pltpu.SMEM), whole, pl.BlockSpec(memory_space=pltpu.HBM)],
        out_specs=[whole, whole],
        scratch_shapes=[pltpu.VMEM(tiles.shape, jnp.float32), pltpu.SemaphoreType.DMA((tiles.shape[0], 8))],
        compiler_params=pltpu.CompilerParams(vmem_limit_bytes=40 * MIB),
        name="split_tiles",
    )(spot, factors, tiles)


def product_kernel(n, spot, high, low, near, far, near_other, far_other, keep, send, panel_high, panel_low):
    zl, y, core = spot[2], spot[3], spot[4]
    for dc, pieces in enumerate(((near, far), (near_other, far_other))):
        order = ring_order(core ^ dc)
        for piece, dys in zip(pieces, (order[:2], order[2:])):
            for part, (dy, dz) in enumerate((dy, dz) for dy in dys for dz in (0, 2, 1, 3)):
                block = ((zl ^ dz) * 4 + (y ^ dy)) * 2 + (core ^ dc)
                rows = pl.ds(pl.multiple_of(block * 64, 64), 64)
                panel_high[rows, :], panel_low[rows, :] = split(piece[pl.ds(part * 64, 64), :])
    dot = functools.partial(jnp.dot, preferred_element_type=jnp.float32)
    step = high.shape[1] // 2
    for half, out in enumerate((keep, send)):
        rows = pl.ds(half * step, step)
        total = dot(low[0, rows, :], panel_high[...])
        total += dot(high[0, rows, :], panel_low[...])
        total += dot(high[0, rows, :], panel_high[...])
        out[...] = total


def product(n, spot, high, low, pieces):
    height, breadth = high.shape[1:]
    width = pieces[0].shape[1]
    whole = pl.BlockSpec(memory_space=pltpu.VMEM)
    tile_spec = pl.BlockSpec((1, height, breadth), lambda i: (n, 0, 0))
    return pl.pallas_call(
        functools.partial(product_kernel, n),
        out_shape=[jax.ShapeDtypeStruct((height // 2, width), jnp.float32)] * 2,
        grid=(1,),
        in_specs=[pl.BlockSpec(memory_space=pltpu.SMEM), tile_spec, tile_spec] + [whole] * len(pieces),
        out_specs=[whole] * 2,
        scratch_shapes=[pltpu.VMEM((breadth, width), jnp.bfloat16)] * 2,
        compiler_params=pltpu.CompilerParams(vmem_limit_bytes=20 * MIB),
        name="product",
    )(spot, high, low, *pieces)


def local(lower_panel, panel_mask, inverse_tiles, tile_mask):
    number = lower_panel.shape[0]
    spot = jnp.stack([lax.axis_index(a) for a in AXES]).astype(jnp.int32)
    factors = -(tile_mask * panel_mask[:, None, :]).astype(jnp.float32)
    factors = jnp.repeat(factors, BLK, axis=2)[:, :, None, :]
    def after(value, *gates):
        return lax.optimization_barrier((value, gates))[0]

    def grow(value, axis, by, name):
        return jnp.concatenate([value, swap(value, axis, by, name)], axis=-2)

    def halves(total):
        half = total.shape[0] // 2
        return total[:half], total[half:]

    def add_half(keep, send, axis, by, name):
        return keep + swap(send, axis, by, name)

    near_z, far_z, first, second, across = (1, 1), (2, 2), (1, 3), (3, 1), (1, 1)

    a0 = grow(lower_panel[0], "zl", far_z, "z_far_0")
    a12 = grow(lower_panel[1:], "zl", far_z, "z_far_12")
    g0 = grow(a0, "zl", near_z, "z_near_0")
    g12 = grow(a12, "zl", near_z, "z_near_12")
    n0 = grow(g0, "y", first, "y_first_0")
    high, low = split_tiles(spot, inverse_tiles, after(factors, n0))
    f0 = swap(n0, "y", second, "y_second_0")
    n12 = grow(after(g12, n0), "y", first, "y_first_12")
    outs0 = product(0, spot, high, low, [n0, f0, swap_core(n0, "core_near_0"), swap_core(after(f0, high), "core_far_0")])
    n1, n2 = n12[0], n12[1]
    f1 = swap(n1, "y", second, "y_second_1")
    f2 = swap(n2, "y", second, "y_second_2")
    x0 = add_half(*outs0, "x", first, "x_first_0")
    c1 = [swap_core(n1, "core_near_1"), swap_core(after(f1, x0), "core_far_1")]
    outs1 = product(1, spot, high, low, [n1, f1, *c1])
    h0 = add_half(*halves(x0), "x", second, "x_second_0")
    x1 = add_half(*outs1, "x", first, "x_first_1")
    c2 = [swap_core(n2, "core_near_2"), swap_core(after(f2, outs1, h0), "core_far_2")]
    outs2 = product(2, spot, high, low, [n2, f2, *c2])
    h1 = add_half(*halves(after(x1, outs2)), "x", second, "x_second_1")
    x2 = add_half(*outs2, "x", first, "x_first_2")
    h01 = jnp.stack([after(h0, outs2), h1])
    r01 = h01[:, :64] + swap(h01[:, 64:], "zh", across, "zh_01")
    h2 = add_half(*halves(x2), "x", second, "x_second_2")
    r2 = add_half(*halves(h2), "zh", across, "zh_2")
    return jnp.concatenate([r01, r2[None]])


def solution(mesh):
    mesh = Mesh(mesh.devices.reshape(SIZES), AXES)
    row, col = AXES[:2], AXES[2:]
    return jax.shard_map(
        local,
        mesh=mesh,
        in_specs=(P(None, AXES, None), P(None, row), P(None, col, row), P(None, col, row)),
        out_specs=P(None, col + row, None),
        check_vma=False,
    )
```

```python
import functools

import jax
import jax.numpy as jnp
from jax import lax
from jax.experimental import pallas as pl
from jax.experimental.pallas import tpu as pltpu
from jax.sharding import Mesh
from jax.sharding import PartitionSpec as P

AXES = ("zh", "x", "zl", "y", "core")
SIZES = (2, 4, 4, 4, 2)
BLK = 128
MIB = 1 << 20


def swap(value, axis, by, name):
    pairs = [(2 * i + core, 2 * (i ^ by[core]) + core) for i in range(SIZES[AXES.index(axis)]) for core in range(2)]
    with jax.named_scope(name):
        return lax.ppermute(value, (axis, "core"), pairs)


def swap_core(value, name):
    with jax.named_scope(name):
        return lax.ppermute(value, "core", [(0, 1), (1, 0)])


def split(value):
    high = value.astype(jnp.bfloat16)
    low = (value - high.astype(jnp.float32)).astype(jnp.bfloat16)
    return high, low


def ring_order(core):
    return [0, 1 + 2 * core, 3 - 2 * core, 2]


def tiles_kernel(spot, factors, tiles, high, low, held, arrived):
    zh, x, core = spot[0], spot[1], spot[4]
    own, first, second, both = ring_order(core)
    sources = [(zh ^ dz) * 4 + (x ^ dx) for dx in (own, second, first, both) for dz in range(2)]
    number, height, _ = tiles.shape
    rows = height // len(sources)

    def copy(n, i):
        rows_from = pl.ds(pl.multiple_of(sources[i] * rows, rows), rows)
        return pltpu.make_async_copy(tiles.at[n, rows_from], held.at[n, pl.ds(i * rows, rows)], arrived.at[n, i])

    @pl.loop(0, number)
    def _(n):
        for i in range(len(sources)):
            copy(n, i).start()

    @pl.loop(0, number)
    def _(n):
        for i, source in enumerate(sources):
            copy(n, i).wait()
            to = pl.ds(i * rows, rows)
            high[n, to], low[n, to] = split(held[n, to] * factors[n, source // 2])


def split_tiles(spot, tiles, factors):
    out = jax.ShapeDtypeStruct(tiles.shape, jnp.bfloat16)
    whole = pl.BlockSpec(memory_space=pltpu.VMEM)
    return pl.pallas_call(
        tiles_kernel,
        out_shape=[out, out],
        in_specs=[pl.BlockSpec(memory_space=pltpu.SMEM), whole, pl.BlockSpec(memory_space=pltpu.HBM)],
        out_specs=[whole, whole],
        scratch_shapes=[pltpu.VMEM(tiles.shape, jnp.float32), pltpu.SemaphoreType.DMA((tiles.shape[0], 8))],
        compiler_params=pltpu.CompilerParams(vmem_limit_bytes=40 * MIB),
        name="split_tiles",
    )(spot, factors, tiles)


def product_kernel(n, spot, high, low, near, far, near_other, far_other, keep, send, panel_high, panel_low):
    zl, y, core = spot[2], spot[3], spot[4]
    for dc, pieces in enumerate(((near, far), (near_other, far_other))):
        order = ring_order(core ^ dc)
        for piece, dys in zip(pieces, (order[:2], order[2:])):
            for part, (dy, dz) in enumerate((dy, dz) for dy in dys for dz in (0, 2, 1, 3)):
                block = ((zl ^ dz) * 4 + (y ^ dy)) * 2 + (core ^ dc)
                rows = pl.ds(pl.multiple_of(block * 64, 64), 64)
                panel_high[rows, :], panel_low[rows, :] = split(piece[pl.ds(part * 64, 64), :])
    dot = functools.partial(jnp.dot, preferred_element_type=jnp.float32)
    step = high.shape[1] // 2
    for half, out in enumerate((keep, send)):
        rows = pl.ds(half * step, step)
        total = dot(low[0, rows, :], panel_high[...])
        total += dot(high[0, rows, :], panel_low[...])
        total += dot(high[0, rows, :], panel_high[...])
        out[...] = total


def product(n, spot, high, low, pieces):
    height, breadth = high.shape[1:]
    width = pieces[0].shape[1]
    whole = pl.BlockSpec(memory_space=pltpu.VMEM)
    tile_spec = pl.BlockSpec((1, height, breadth), lambda i: (n, 0, 0))
    return pl.pallas_call(
        functools.partial(product_kernel, n),
        out_shape=[jax.ShapeDtypeStruct((height // 2, width), jnp.float32)] * 2,
        grid=(1,),
        in_specs=[pl.BlockSpec(memory_space=pltpu.SMEM), tile_spec, tile_spec] + [whole] * len(pieces),
        out_specs=[whole] * 2,
        scratch_shapes=[pltpu.VMEM((breadth, width), jnp.bfloat16)] * 2,
        compiler_params=pltpu.CompilerParams(vmem_limit_bytes=20 * MIB),
        name="product",
    )(spot, high, low, *pieces)


def local(lower_panel, panel_mask, inverse_tiles, tile_mask):
    number = lower_panel.shape[0]
    spot = jnp.stack([lax.axis_index(a) for a in AXES]).astype(jnp.int32)
    factors = -(tile_mask * panel_mask[:, None, :]).astype(jnp.float32)
    factors = jnp.repeat(factors, BLK, axis=2)[:, :, None, :]
    def after(value, *gates):
        return lax.optimization_barrier((value, gates))[0]

    def grow(value, axis, by, name):
        return jnp.concatenate([value, swap(value, axis, by, name)], axis=-2)

    def halves(total):
        half = total.shape[0] // 2
        return total[:half], total[half:]

    def add_half(keep, send, axis, by, name):
        return keep + swap(send, axis, by, name)

    near_z, far_z, first, second, across = (1, 1), (2, 2), (1, 3), (3, 1), (1, 1)

    own = lower_panel[0]
    g0 = jnp.concatenate([own] + [swap(own, "zl", (dz, dz), "z_{}_0".format(dz)) for dz in (2, 1, 3)])
    a12 = grow(lower_panel[1:], "zl", far_z, "z_far_12")
    g12 = grow(a12, "zl", near_z, "z_near_12")
    n0 = grow(g0, "y", first, "y_first_0")
    high, low = split_tiles(spot, inverse_tiles, after(factors, n0))
    f0 = swap(n0, "y", second, "y_second_0")
    n12 = grow(after(g12, n0), "y", first, "y_first_12")
    outs0 = product(0, spot, high, low, [n0, f0, swap_core(n0, "core_near_0"), swap_core(after(f0, high), "core_far_0")])
    n1, n2 = n12[0], n12[1]
    f1 = swap(n1, "y", second, "y_second_1")
    f2 = swap(n2, "y", second, "y_second_2")
    x0 = add_half(*outs0, "x", first, "x_first_0")
    c1 = [swap_core(n1, "core_near_1"), swap_core(after(f1, x0), "core_far_1")]
    outs1 = product(1, spot, high, low, [n1, f1, *c1])
    h0 = add_half(*halves(x0), "x", second, "x_second_0")
    x1 = add_half(*outs1, "x", first, "x_first_1")
    c2 = [swap_core(n2, "core_near_2"), swap_core(after(f2, outs1), "core_far_2")]
    outs2 = product(2, spot, high, low, [n2, f2, *c2])
    h1 = add_half(*halves(after(x1, outs2)), "x", second, "x_second_1")
    x2 = add_half(*outs2, "x", first, "x_first_2")
    h01 = jnp.stack([after(h0, outs2), h1])
    r01 = h01[:, :64] + swap(h01[:, 64:], "zh", across, "zh_01")
    h2 = add_half(*halves(x2), "x", second, "x_second_2")
    r2 = add_half(*halves(h2), "zh", across, "zh_2")
    return jnp.concatenate([r01, r2[None]])


def solution(mesh):
    mesh = Mesh(mesh.devices.reshape(SIZES), AXES)
    row, col = AXES[:2], AXES[2:]
    return jax.shard_map(
        local,
        mesh=mesh,
        in_specs=(P(None, AXES, None), P(None, row), P(None, col, row), P(None, col, row)),
        out_specs=P(None, col + row, None),
        check_vma=False,
    )
```

```python
import functools

import jax
import jax.numpy as jnp
from jax import lax
from jax.experimental import pallas as pl
from jax.experimental.pallas import tpu as pltpu
from jax.sharding import Mesh
from jax.sharding import PartitionSpec as P

AXES = ("zh", "x", "zl", "y", "core")
SIZES = (2, 4, 4, 4, 2)
BLK = 128
MIB = 1 << 20


def swap(value, axis, by, name):
    pairs = [(2 * i + core, 2 * (i ^ by[core]) + core) for i in range(SIZES[AXES.index(axis)]) for core in range(2)]
    with jax.named_scope(name):
        return lax.ppermute(value, (axis, "core"), pairs)


def swap_core(value, name):
    with jax.named_scope(name):
        return lax.ppermute(value, "core", [(0, 1), (1, 0)])


def split(value):
    high = value.astype(jnp.bfloat16)
    low = (value - high.astype(jnp.float32)).astype(jnp.bfloat16)
    return high, low


def ring_order(core):
    return [0, 1 + 2 * core, 3 - 2 * core, 2]


def tiles_kernel(spot, factors, tiles, high, low, held, arrived):
    zh, x, core = spot[0], spot[1], spot[4]
    own, first, second, both = ring_order(core)
    sources = [(zh ^ dz) * 4 + (x ^ dx) for dx in (own, second, first, both) for dz in range(2)]
    number, height, _ = tiles.shape
    rows = height // len(sources)

    def copy(n, i):
        rows_from = pl.ds(pl.multiple_of(sources[i] * rows, rows), rows)
        return pltpu.make_async_copy(tiles.at[n, rows_from], held.at[n, pl.ds(i * rows, rows)], arrived.at[n, i])

    @pl.loop(0, number)
    def _(n):
        for i in range(len(sources)):
            copy(n, i).start()

    @pl.loop(0, number)
    def _(n):
        for i, source in enumerate(sources):
            copy(n, i).wait()
            to = pl.ds(i * rows, rows)
            high[n, to], low[n, to] = split(held[n, to] * factors[n, source // 2])


def split_tiles(spot, tiles, factors):
    out = jax.ShapeDtypeStruct(tiles.shape, jnp.bfloat16)
    whole = pl.BlockSpec(memory_space=pltpu.VMEM)
    return pl.pallas_call(
        tiles_kernel,
        out_shape=[out, out],
        in_specs=[pl.BlockSpec(memory_space=pltpu.SMEM), whole, pl.BlockSpec(memory_space=pltpu.HBM)],
        out_specs=[whole, whole],
        scratch_shapes=[pltpu.VMEM(tiles.shape, jnp.float32), pltpu.SemaphoreType.DMA((tiles.shape[0], 8))],
        compiler_params=pltpu.CompilerParams(vmem_limit_bytes=40 * MIB),
        name="split_tiles",
    )(spot, factors, tiles)


def product_kernel(n, spot, high, low, near, far, near_other, far_other, keep, send, panel_high, panel_low):
    zl, y, core = spot[2], spot[3], spot[4]
    for dc, pieces in enumerate(((near, far), (near_other, far_other))):
        order = ring_order(core ^ dc)
        for piece, dys in zip(pieces, (order[:2], order[2:])):
            for part, (dy, dz) in enumerate((dy, dz) for dy in dys for dz in (0, 2, 1, 3)):
                block = ((zl ^ dz) * 4 + (y ^ dy)) * 2 + (core ^ dc)
                rows = pl.ds(pl.multiple_of(block * 64, 64), 64)
                panel_high[rows, :], panel_low[rows, :] = split(piece[pl.ds(part * 64, 64), :])
    dot = functools.partial(jnp.dot, preferred_element_type=jnp.float32)
    step = high.shape[1] // 2
    for half, out in enumerate((keep, send)):
        rows = pl.ds(half * step, step)
        total = dot(low[0, rows, :], panel_high[...])
        total += dot(high[0, rows, :], panel_low[...])
        total += dot(high[0, rows, :], panel_high[...])
        out[...] = total


def product(n, spot, high, low, pieces):
    height, breadth = high.shape[1:]
    width = pieces[0].shape[1]
    whole = pl.BlockSpec(memory_space=pltpu.VMEM)
    tile_spec = pl.BlockSpec((1, height, breadth), lambda i: (n, 0, 0))
    return pl.pallas_call(
        functools.partial(product_kernel, n),
        out_shape=[jax.ShapeDtypeStruct((height // 2, width), jnp.float32)] * 2,
        grid=(1,),
        in_specs=[pl.BlockSpec(memory_space=pltpu.SMEM), tile_spec, tile_spec] + [whole] * len(pieces),
        out_specs=[whole] * 2,
        scratch_shapes=[pltpu.VMEM((breadth, width), jnp.bfloat16)] * 2,
        compiler_params=pltpu.CompilerParams(vmem_limit_bytes=20 * MIB),
        name="product",
    )(spot, high, low, *pieces)


def local(lower_panel, panel_mask, inverse_tiles, tile_mask):
    number = lower_panel.shape[0]
    spot = jnp.stack([lax.axis_index(a) for a in AXES]).astype(jnp.int32)
    factors = -(tile_mask * panel_mask[:, None, :]).astype(jnp.float32)
    factors = jnp.repeat(factors, BLK, axis=2)[:, :, None, :]
    def after(value, *gates):
        return lax.optimization_barrier((value, gates))[0]

    def grow(value, axis, by, name):
        return jnp.concatenate([value, swap(value, axis, by, name)], axis=-2)

    def halves(total):
        half = total.shape[0] // 2
        return total[:half], total[half:]

    def add_half(keep, send, axis, by, name):
        return keep + swap(send, axis, by, name)

    near_z, far_z, first, second, across = (1, 1), (2, 2), (1, 3), (3, 1), (1, 1)

    own = lower_panel[0]
    far = swap(lower_panel, "zl", far_z, "z_far")
    z1, z3 = swap(own, "zl", (1, 1), "z_1_0"), swap(own, "zl", (3, 3), "z_3_0")
    g0 = jnp.concatenate([own, far[0], z1, z3])
    a12 = jnp.concatenate([lower_panel[1:], far[1:]], axis=1)
    g12 = grow(a12, "zl", near_z, "z_near_12")
    n0 = grow(g0, "y", first, "y_first_0")
    high, low = split_tiles(spot, inverse_tiles, after(factors, n0))
    f0 = swap(n0, "y", second, "y_second_0")
    n12 = grow(after(g12, n0), "y", first, "y_first_12")
    outs0 = product(0, spot, high, low, [n0, f0, swap_core(n0, "core_near_0"), swap_core(after(f0, high), "core_far_0")])
    n1, n2 = n12[0], n12[1]
    f1 = swap(n1, "y", second, "y_second_1")
    f2 = swap(n2, "y", second, "y_second_2")
    x0 = add_half(*outs0, "x", first, "x_first_0")
    c1 = [swap_core(n1, "core_near_1"), swap_core(after(f1, x0), "core_far_1")]
    outs1 = product(1, spot, high, low, [n1, f1, *c1])
    h0 = add_half(*halves(x0), "x", second, "x_second_0")
    x1 = add_half(*outs1, "x", first, "x_first_1")
    c2 = [swap_core(n2, "core_near_2"), swap_core(after(f2, outs1), "core_far_2")]
    outs2 = product(2, spot, high, low, [n2, f2, *c2])
    h1 = add_half(*halves(after(x1, outs2)), "x", second, "x_second_1")
    x2 = add_half(*outs2, "x", first, "x_first_2")
    h01 = jnp.stack([after(h0, outs2), h1])
    r01 = h01[:, :64] + swap(h01[:, 64:], "zh", across, "zh_01")
    h2 = add_half(*halves(x2), "x", second, "x_second_2")
    r2 = add_half(*halves(h2), "zh", across, "zh_2")
    return jnp.concatenate([r01, r2[None]])


def solution(mesh):
    mesh = Mesh(mesh.devices.reshape(SIZES), AXES)
    row, col = AXES[:2], AXES[2:]
    return jax.shard_map(
        local,
        mesh=mesh,
        in_specs=(P(None, AXES, None), P(None, row), P(None, col, row), P(None, col, row)),
        out_specs=P(None, col + row, None),
        check_vma=False,
    )
```
